32 devices in a mesh: groups: 2 (over x), row: 8 (over z, y), col: 2 (over core).
Axes of the slice: x: 2, y: 2, z: 4, core: 2. Of those that a mesh axis runs over, the one named last changes fastest.
Arguments:
- sky_map: bfloat16 [512, 1024, 128], P(('groups', 'row'), 'col'), parts along dimension 0, may hold values from -6 to 6
- expand_weight: bfloat16 [128, 256], replicated, may hold values from -0.5 to 0.5
- expand_bias: float32 [256], replicated, may hold values from -3 to 3
- depth_weight: float32 [3, 3, 256], replicated, may hold values from -2 to 2
- depth_bias: float32 [256], replicated, may hold values from -3 to 3
- project_weight: bfloat16 [256, 128], replicated, may hold values from -0.375 to 0.375
- project_bias: float32 [128], replicated, may hold values from -3 to 3
- norm_gain: float32 [128], replicated, may hold values from 0.1 to 1.9
- norm_bias: float32 [128], replicated, may hold values from -3 to 3
- mixing_weight: bfloat16 [128, 384], replicated
- position_bias: float32 [4, 225], replicated, may hold values from -4 to 4
- output_weight: bfloat16 [128, 128], replicated, may hold values from -0.5 to 0.5
Outputs:
- block_out: bfloat16 [512, 1024, 128], P(('groups', 'row'), 'col'), parts along dimension 0
The draws below stay inside these ranges and needn't reach their ends.
There are 2 independent parts, one for each index of `groups`. The reference program is written for one: setup_inputs(seed, part) draws one part's arguments, and reference() takes and returns one part's arrays. A program takes and returns all parts, laid end to end along the dimension named above; an argument that names none is the same for every part. Nothing has to cross between parts.
All inputs are finite; a program needn't handle non-finite values.
Results may differ from the reference program's by a relative error of at most 0.023.
Values may be sent and summed in bfloat16 or wider, within the bound.
A program may use at most 128 MiB of HBM per device.

```python
import jax
import jax.numpy as jnp
from jax import lax

CH = 128
EXP_CH = 256
HEADS = 4
G = 8
MAP_ROWS = 256
MAP_COLS = 1024


def draw_mixing_weight(key, part):
    first_key = jax.random.fold_in(jax.random.fold_in(key, 7), 0)
    base = jax.random.normal(first_key, (CH, 3 * CH), jnp.float32) * CH ** (-0.5)
    return base.astype(jnp.bfloat16)


def levels(key, dims, cuts, smallest, top_value):
    loudness, own = 1.0, jax.random.fold_in(key, 6)
    for dim, blocks in cuts:
        heights = jnp.exp(jax.random.uniform(jax.random.fold_in(own, dim), (blocks,), jnp.float32, smallest / len(cuts), top_value / len(cuts)))
        loudness = loudness * jnp.repeat(heights, dims[dim] // blocks).reshape([-1 if axis == dim else 1 for axis in range(len(dims))])
    return loudness


def noise(stream_key, extent, width, most, shards=(), kind=jnp.bfloat16):
    values = jax.random.normal(stream_key, extent, jnp.float32) * width
    if len(shards) > 0:
        values = levels(stream_key, extent, shards, -0.22, 0.18) * values
    return jnp.clip(values, min=-most, max=most).astype(kind)


def setup_inputs(seed: int = 0, part: int = 0) -> dict:
    key_list = jax.random.split(jax.random.key(seed), 13)
    part_splits = jax.random.split(jax.random.fold_in(key_list[12], part), 13)
    return {
        "sky_map": noise(part_splits[0], (MAP_ROWS, MAP_COLS, CH), 1.0, 6.0, ((0, 8), (1, 2))),
        "expand_weight": noise(key_list[1], (CH, EXP_CH), CH ** -0.5, 0.5),
        "expand_bias": noise(key_list[2], (EXP_CH,), 0.5, 3.0, (), jnp.float32),
        "depth_weight": noise(key_list[3], (3, 3, EXP_CH), 9 ** -0.5, 2.0, (), jnp.float32),
        "depth_bias": noise(key_list[4], (EXP_CH,), 0.5, 3.0, (), jnp.float32),
        "project_weight": noise(key_list[5], (EXP_CH, CH), EXP_CH ** -0.5, 0.375),
        "project_bias": noise(key_list[6], (CH,), 0.5, 3.0, (), jnp.float32),
        "norm_gain": jnp.clip(1.0 + 0.18 * jax.random.normal(key_list[7], (CH,), jnp.float32), 0.1, 1.9),
        "norm_bias": noise(key_list[8], (CH,), 0.5, 3.0, (), jnp.float32),
        "mixing_weight": draw_mixing_weight(jax.random.fold_in(key_list[12], 71), part),
        "position_bias": noise(key_list[10], (HEADS, (2 * G - 1) * (2 * G - 1)), 1.0, 4.0, (), jnp.float32),
        "output_weight": noise(key_list[11], (CH, CH), CH ** -0.5, 0.5),
    }


def gelu_tanh(values):
    return jax.nn.gelu(values, approximate=True)

def expand_layer(features, expand_weight, expand_bias):
    return gelu_tanh(jnp.dot(features, expand_weight, preferred_element_type=jnp.float32) + expand_bias).astype(jnp.bfloat16)

def depthwise(padded, depth_weight, depth_bias, row_count, col_count):
    accumulated = jnp.zeros((row_count, col_count, padded.shape[2]), jnp.float32) + depth_bias
    for row_shift in range(3):
        for col_shift in range(3):
            accumulated = accumulated + padded[row_shift:row_shift + row_count, col_shift:col_shift + col_count].astype(jnp.float32) * depth_weight[row_shift, col_shift]
    return gelu_tanh(accumulated).astype(jnp.bfloat16)

def layer_norm(features, norm_gain, norm_bias):
    values = features.astype(jnp.float32)
    mean_value = lax.optimization_barrier(jnp.mean(values, axis=-1, keepdims=True))
    variance = lax.optimization_barrier(jnp.mean((values - mean_value) ** 2, axis=-1, keepdims=True))
    return ((values - mean_value) * lax.rsqrt(variance + 1e-05) * norm_gain + norm_bias).astype(jnp.bfloat16)

def grid_bias(position_bias, grid_side):
    position = jnp.arange(grid_side * grid_side, dtype=jnp.int32)
    row_of = position // grid_side
    col_of = position % grid_side
    offset_index = (row_of[:, None] - row_of[None, :] + grid_side - 1) * (2 * grid_side - 1) + (col_of[:, None] - col_of[None, :] + grid_side - 1)
    entries = jnp.arange((2 * grid_side - 1) ** 2, dtype=jnp.int32)
    one_hot = (offset_index[:, :, None] == entries[None, None, :]).astype(jnp.float32)
    return jnp.einsum('qkt,ht->hqk', one_hot, position_bias.astype(jnp.float32), precision=lax.Precision.HIGHEST)

def attend(projected, table, head_count):
    group_count, tokens, triple = projected.shape
    channels = triple // 3
    head_size = channels // head_count
    split_parts = projected.reshape(group_count, tokens, 3, head_count, head_size).astype(jnp.float32)
    query_part = split_parts[:, :, 0]
    key_part = split_parts[:, :, 1]
    value_part = split_parts[:, :, 2]
    scores = jnp.einsum('nqhd,nkhd->nhqk', query_part, key_part) * head_size ** (-0.5) + table[None]
    probs = jax.nn.softmax(scores, axis=-1).astype(jnp.bfloat16)
    attended = jnp.einsum('nhqk,nkhd->nqhd', probs.astype(jnp.float32), value_part)
    return attended.astype(jnp.bfloat16).reshape(group_count, tokens, channels)

def reference(sky_map, expand_weight, expand_bias, depth_weight, depth_bias, project_weight, project_bias, norm_gain, norm_bias, mixing_weight, position_bias, output_weight):
    map_rows, map_cols, channels = sky_map.shape
    expanded = expand_layer(sky_map, expand_weight, expand_bias)
    padded = jnp.pad(expanded, ((1, 1), (1, 1), (0, 0)))
    hidden = depthwise(padded, depth_weight, depth_bias, map_rows, map_cols)
    after_conv = (sky_map.astype(jnp.float32) + jnp.dot(hidden, project_weight, preferred_element_type=jnp.float32) + project_bias).astype(jnp.bfloat16)
    normed = layer_norm(after_conv, norm_gain, norm_bias)
    projected = jnp.dot(normed, mixing_weight, preferred_element_type=jnp.float32).astype(jnp.bfloat16)
    stride_rows = map_rows // G
    stride_cols = map_cols // G
    grouped = projected.reshape(G, stride_rows, G, stride_cols, 3 * channels).transpose(1, 3, 0, 2, 4).reshape(stride_rows, stride_cols, G * G, 3 * channels)
    table = grid_bias(position_bias, G)

    def one_block(block):
        return attend(block, table, HEADS)
    heads_out = lax.map(one_block, grouped)
    returned = heads_out.reshape(stride_rows, stride_cols, G, G, channels).transpose(2, 0, 3, 1, 4).reshape(map_rows, map_cols, channels)
    return (after_conv.astype(jnp.float32) + jnp.dot(returned, output_weight, preferred_element_type=jnp.float32)).astype(jnp.bfloat16)
```

```python
import functools
import math

import jax
import jax.numpy as jnp
from jax import lax
from jax.experimental import pallas as pl
from jax.experimental.pallas import tpu as pltpu
from jax.sharding import PartitionSpec as P

HEADS = 4
G = 8
EDGE = 16
LOG2E = math.log2(math.e)
MESH = pl.DeviceIdType.MESH
F32 = jnp.float32
BF16 = jnp.bfloat16


def gelu_tanh(values):
    half = 0.5 * values
    c0 = math.sqrt(2.0 / math.pi)
    return half * jnp.tanh(values * (c0 + (c0 * 0.044715) * (values * values))) + half


def kernel(
    sizes,
    sky,
    expand_weight,
    expand_bias,
    depth_weight,
    depth_bias,
    project_weight,
    project_bias,
    norm_gain,
    norm_bias,
    mixing_weight,
    table,
    head_mask,
    output_weight,
    out,
    halo_rows,
    halo_cols,
    expanded,
    side,
    t_left,
    t_mid,
    t_right,
    hidden,
    normed,
    received,
    group_in,
    group_out,
    attended,
    returned,
    halo_send,
    halo_recv,
    forward_send,
    forward_recv,
    back_send,
    back_recv,
):
    row_size, col_size = sizes
    rows, cols, channels = sky.shape
    chunks = rows // G
    across = G // col_size
    stride = cols // across
    width = stride // col_size
    tokens = G * G
    slots = G * col_size
    repeat = row_size // G

    face = lax.axis_index("groups")
    row = lax.axis_index("row")
    col = lax.axis_index("col")
    other = 1 - col
    my_p = row // repeat
    parity = row % repeat
    me = my_p * col_size + col
    has_up = row > 0
    has_down = row < row_size - 1

    def partner(j):
        slot = (me + 8 + ((j + 1) // 2) * (2 * (j % 2) - 1)) % slots
        p, c = slot // col_size, slot % col_size
        return slot, p, c, (face, p * repeat + parity, c)

    barrier = pltpu.get_barrier_semaphore()

    def greet(j, carry):
        pl.semaphore_signal(barrier, inc=1, device_id=partner(j)[3], device_id_type=MESH)
        return carry

    lax.fori_loop(0, slots - 1, greet, 0)
    pl.semaphore_wait(barrier, slots - 1)
    if repeat > 1:
        for there, near in ((has_up, row - 1), (has_down, row + 1)):

            @pl.when(there)
            def _():
                for c in (col, other):
                    pl.semaphore_signal(barrier, inc=1, device_id=(face, near, c), device_id_type=MESH)

        for there in (has_up, has_down):

            @pl.when(there)
            def _():
                pl.semaphore_wait(barrier, 2)

    edge_start = pl.multiple_of(other * (cols - EDGE), EDGE)
    edge = pl.ds(edge_start, EDGE)

    def remote(src, dst, i, j, device):
        return pltpu.make_async_remote_copy(
            src_ref=src,
            dst_ref=dst,
            send_sem=halo_send.at[i],
            recv_sem=halo_recv.at[j],
            device_id=device,
            device_id_type=MESH,
        )

    up_row = remote(sky.at[0], halo_rows.at[1], 0, 1, (face, row - 1, col))
    up_corner = remote(sky.at[0, edge], halo_cols.at[rows + 1], 1, 4, (face, row - 1, other))
    down_row = remote(sky.at[rows - 1], halo_rows.at[0], 2, 0, (face, row + 1, col))
    down_corner = remote(sky.at[rows - 1, edge], halo_cols.at[0], 3, 3, (face, row + 1, other))
    side_copy = remote(sky.at[:, edge], halo_cols.at[pl.ds(1, rows)], 4, 2, (face, row, other))

    @pl.when(has_up)
    def _():
        up_row.start()
        up_corner.start()

    @pl.when(has_down)
    def _():
        down_row.start()
        down_corner.start()

    side_copy.start()

    def expand(features):
        return gelu_tanh(
            jnp.dot(features, expand_weight[...], preferred_element_type=F32) + expand_bias[...]
        ).astype(BF16)

    def put_row(i, values):
        expanded[0, i] = values[:, :128]
        expanded[1, i] = values[:, 128:]

    def expand_row(i, carry):
        put_row(i + 1, expand(sky[i]))
        return carry

    lax.fori_loop(0, rows, expand_row, 0)

    side_copy.wait_recv()
    strip = expand(halo_cols[1 : rows + 1].reshape(rows * EDGE, channels)).astype(F32)
    side[0, 1 : rows + 1] = strip[:, :128].reshape(rows, EDGE, 128)
    side[1, 1 : rows + 1] = strip[:, 128:].reshape(rows, EDGE, 128)
    for there, slot, at, row_copy, corner_copy in (
        (has_up, 0, 0, down_row, down_corner),
        (has_down, 1, rows + 1, up_row, up_corner),
    ):

        @pl.when(there)
        def _():
            row_copy.wait_recv()
            corner_copy.wait_recv()
            put_row(at, expand(halo_rows[slot]))
            corner = expand(halo_cols[at]).astype(F32)
            side[0, at] = corner[:, :128]
            side[1, at] = corner[:, 128:]

        @pl.when(jnp.logical_not(there))
        def _():
            put_row(at, jnp.zeros((cols, 256), BF16))
            side[:, at] = jnp.zeros((2, EDGE, 128), F32)

    edge_at = other * 0 + col * (EDGE - 1)
    on_left = col.astype(F32)
    on_right = 1.0 - on_left
    tile = 128

    def conv_row(k, d):
        i = d * chunks + k
        for h in range(2):
            lanes = slice(h * 128, h * 128 + 128)
            taps = [[depth_weight[3 * a + b : 3 * a + b + 1, lanes] for b in range(3)] for a in range(3)]
            for j in range(0, cols, tile):
                cells = [expanded[h, i + a, j : j + tile, :].astype(F32) for a in range(3)]
                for b, buffer in ((0, t_left), (1, t_mid), (2, t_right)):
                    buffer[h, 8 + j : 8 + j + tile] = (
                        cells[0] * taps[0][b] + cells[1] * taps[1][b] + cells[2] * taps[2][b]
                    )
            beyond = [side[h, i + a, pl.ds(edge_at, 1), :] for a in range(3)]
            for b, buffer, at, on in ((0, t_left, 7, on_left), (2, t_right, 8 + cols, on_right)):
                buffer[h, at : at + 1] = on * (
                    beyond[0] * taps[0][b] + beyond[1] * taps[1][b] + beyond[2] * taps[2][b]
                )
            for j in range(0, cols, tile):
                total = (
                    t_left[h, 7 + j : 7 + j + tile]
                    + t_mid[h, 8 + j : 8 + j + tile]
                    + t_right[h, 9 + j : 9 + j + tile]
                    + depth_bias[:, lanes]
                )
                hidden[j : j + tile, lanes] = gelu_tanh(total).astype(BF16)
        for j in range(0, cols, tile):
            after = (
                sky[i, j : j + tile].astype(F32)
                + jnp.dot(hidden[j : j + tile], project_weight[...], preferred_element_type=F32)
                + project_bias[...]
            ).astype(BF16)
            out[i, j : j + tile] = after
            values = after.astype(F32)
            centred = values - jnp.mean(values, axis=-1, keepdims=True)
            variance = jnp.mean(centred * centred, axis=-1, keepdims=True)
            normed[k, d, j // stride, j % stride : j % stride + tile] = (
                centred * lax.rsqrt(variance + 1e-05) * norm_gain[...] + norm_bias[...]
            ).astype(BF16)

    def forward_copy(k, j):
        _, p, c, device = partner(j)
        return pltpu.make_async_remote_copy(
            src_ref=normed.at[k, p, :, pl.ds(pl.multiple_of(c * width, width), width)],
            dst_ref=received.at[k, me],
            send_sem=forward_send.at[k],
            recv_sem=forward_recv.at[k],
            device_id=device,
            device_id_type=MESH,
        )

    my_cols = pl.ds(pl.multiple_of(col * width, width), width)

    def back_copy(k, j):
        slot, _, _, device = partner(j)
        return pltpu.make_async_remote_copy(
            src_ref=attended.at[k, slot],
            dst_ref=returned.at[k, my_p, :, my_cols],
            send_sem=back_send.at[k],
            recv_sem=back_recv.at[k],
            device_id=device,
            device_id_type=MESH,
        )

    def conv_chunk(k, carry):
        def one(d, inner):
            conv_row(k, d)
            return inner

        lax.fori_loop(0, G, one, 0)

        def send(j, inner):
            forward_copy(k, j).start()
            return inner

        lax.fori_loop(0, slots - 1, send, 0)
        pltpu.make_async_copy(
            normed.at[k, my_p, :, my_cols], received.at[k, me], forward_recv.at[k]
        ).start()
        return carry

    lax.fori_loop(0, chunks, conv_chunk, 0)

    scale = LOG2E / math.sqrt(channels // HEADS)
    bundle = 8

    def attend_pair(first, second):
        keys, queries, values = [], [], []
        zero = jnp.zeros((tokens, channels), BF16)
        for projected in (first, second):
            key = projected[:, channels : 2 * channels]
            value = projected[:, 2 * channels :]
            keys.append(jnp.concatenate([key] * HEADS, axis=0) * head_mask[...])
            values.append(jnp.concatenate([value] * HEADS, axis=0) * head_mask[...])
        queries = jnp.concatenate(
            [
                jnp.concatenate([first[:, :channels], zero], axis=1),
                jnp.concatenate([zero, second[:, :channels]], axis=1),
            ],
            axis=0,
        )
        scores = lax.dot_general(
            jnp.concatenate(keys, axis=1),
            queries,
            (((1,), (1,)), ((), ())),
            preferred_element_type=F32,
        )
        scores = (scores * scale + table[...]).reshape(HEADS, tokens, 2 * tokens)
        powers = jnp.exp2(scores - jnp.max(scores, axis=1, keepdims=True))
        probs = powers * (1.0 / jnp.sum(powers, axis=1, keepdims=True))
        result = lax.dot_general(
            probs.astype(BF16).reshape(HEADS * tokens, 2 * tokens),
            jnp.concatenate(values, axis=1),
            (((0,), (0,)), ((), ())),
            preferred_element_type=F32,
        )
        return result[:tokens, :channels], result[tokens:, channels:]

    def attend_chunk(k, carry):
        pltpu.make_async_copy(received.at[k], received.at[k], forward_recv.at[k]).wait()

        def widen(s, inner):
            group_in[pl.ds(pl.multiple_of(s * across * width, across * width), across * width)] = (
                received[k, s].reshape(across * width, channels).astype(F32)
            )
            return inner

        lax.fori_loop(0, slots, widen, 0)

        def some_groups(b, inner):
            start = b * bundle
            features = jnp.concatenate(
                [group_in[pl.ds(start + n, tokens, stride=width), :] for n in range(bundle)], axis=0
            ).astype(BF16)
            projected = jnp.dot(features, mixing_weight[...], preferred_element_type=F32).astype(BF16)
            parts = [projected[n * tokens : (n + 1) * tokens] for n in range(bundle)]
            for n in range(0, bundle, 2):
                first, second = attend_pair(parts[n], parts[n + 1])
                group_out[pl.ds(start + n, tokens, stride=width), :] = first
                group_out[pl.ds(start + n + 1, tokens, stride=width), :] = second
            return inner

        lax.fori_loop(0, width // bundle, some_groups, 0)

        def narrow(s, inner):
            attended[k, s] = (
                group_out[pl.ds(pl.multiple_of(s * across * width, across * width), across * width)]
                .astype(BF16)
                .reshape(across, width, channels)
            )
            return inner

        lax.fori_loop(0, slots, narrow, 0)

        def send(j, inner):
            back_copy(k, j).start()
            return inner

        lax.fori_loop(0, slots - 1, send, 0)
        pltpu.make_async_copy(
            attended.at[k, me], returned.at[k, my_p, :, my_cols], back_recv.at[k]
        ).start()
        return carry

    lax.fori_loop(0, chunks, attend_chunk, 0)

    def finish_chunk(k, carry):
        pltpu.make_async_copy(returned.at[k], returned.at[k], back_recv.at[k]).wait()

        def one(d, inner):
            i = d * chunks + k
            out[i] = (
                out[i].astype(F32)
                + jnp.dot(
                    returned[k, d].reshape(cols, channels),
                    output_weight[...],
                    preferred_element_type=F32,
                )
            ).astype(BF16)
            return inner

        lax.fori_loop(0, G, one, 0)
        return carry

    lax.fori_loop(0, chunks, finish_chunk, 0)

    def drain(k, carry):
        sent = received.at[k, pl.ds(0, slots - 1)]
        pltpu.make_async_copy(sent, sent, forward_send.at[k]).wait()
        pltpu.make_async_copy(sent, sent, back_send.at[k]).wait()
        return carry

    lax.fori_loop(0, chunks, drain, 0)

    @pl.when(has_up)
    def _():
        up_row.wait_send()
        up_corner.wait_send()

    @pl.when(has_down)
    def _():
        down_row.wait_send()
        down_corner.wait_send()

    side_copy.wait_send()


def bias_table(position_bias):
    position = jnp.arange(G * G, dtype=jnp.int32)
    p, q = position // G, position % G
    offset = (p[None, :] - p[:, None] + G - 1) * (2 * G - 1) + (q[None, :] - q[:, None] + G - 1)
    entries = jnp.arange((2 * G - 1) ** 2, dtype=jnp.int32)
    one_hot = (offset[:, :, None] == entries[None, None, :]).astype(F32)
    table = jnp.einsum("ktn,hn->hkt", one_hot, position_bias, precision=lax.Precision.HIGHEST)
    table = table.reshape(-1, G * G) * LOG2E
    return jnp.concatenate([table, table], axis=1)


def body(
    sizes,
    sky_map,
    expand_weight,
    expand_bias,
    depth_weight,
    depth_bias,
    project_weight,
    project_bias,
    norm_gain,
    norm_bias,
    mixing_weight,
    position_bias,
    output_weight,
):
    rows, cols, channels = sky_map.shape
    wide = expand_weight.shape[1]
    col_size = sizes[1]
    chunks = rows // G
    across = G // col_size
    stride = cols // across
    width = stride // col_size
    slots = G * col_size
    tokens = G * G
    head_of = jnp.arange(HEADS * tokens, dtype=jnp.int32) // tokens
    lane_head = jnp.arange(channels, dtype=jnp.int32) // (channels // HEADS)
    head_mask = (head_of[:, None] == lane_head[None, :]).astype(BF16)
    vmem = pl.BlockSpec(memory_space=pltpu.VMEM)
    dma = pltpu.SemaphoreType.DMA
    return pl.pallas_call(
        functools.partial(kernel, sizes),
        out_shape=jax.ShapeDtypeStruct(sky_map.shape, BF16),
        in_specs=[vmem] * 13,
        out_specs=vmem,
        scratch_shapes=[
            pltpu.VMEM((2, cols, channels), BF16),
            pltpu.VMEM((rows + 2, EDGE, channels), BF16),
            pltpu.VMEM((2, rows + 2, cols, 128), BF16),
            pltpu.VMEM((2, rows + 2, EDGE, 128), F32),
            pltpu.VMEM((2, cols + 16, 128), F32),
            pltpu.VMEM((2, cols + 16, 128), F32),
            pltpu.VMEM((2, cols + 16, 128), F32),
            pltpu.VMEM((cols, wide), BF16),
            pltpu.VMEM((chunks, G, across, stride, channels), BF16),
            pltpu.VMEM((chunks, slots, across, width, channels), BF16),
            pltpu.VMEM((tokens * width, channels), F32),
            pltpu.VMEM((tokens * width, channels), F32),
            pltpu.VMEM((chunks, slots, across, width, channels), BF16),
            pltpu.VMEM((chunks, G, across, stride, channels), BF16),
            dma((5,)),
            dma((5,)),
            dma((chunks,)),
            dma((chunks,)),
            dma((chunks,)),
            dma((chunks,)),
        ],
        compiler_params=pltpu.CompilerParams(
            collective_id=0, has_side_effects=True, vmem_limit_bytes=58 * 1024 * 1024
        ),
    )(
        sky_map,
        expand_weight,
        expand_bias.reshape(1, wide),
        depth_weight.reshape(9, wide),
        depth_bias.reshape(1, wide),
        project_weight,
        project_bias.reshape(1, channels),
        norm_gain.reshape(1, channels),
        norm_bias.reshape(1, channels),
        mixing_weight,
        bias_table(position_bias),
        head_mask,
        output_weight,
    )


def solution(mesh):
    placed = (P(("groups", "row"), "col", None),) + (P(),) * 11
    sizes = (mesh.shape["row"], mesh.shape["col"])
    return jax.shard_map(
        functools.partial(body, sizes),
        mesh=mesh,
        in_specs=placed,
        out_specs=P(("groups", "row"), "col", None),
        check_vma=False,
    )
```

```python
import functools
import math

import jax
import jax.numpy as jnp
from jax import lax
from jax.experimental import pallas as pl
from jax.experimental.pallas import tpu as pltpu
from jax.sharding import PartitionSpec as P

HEADS = 4
G = 8
EDGE = 16
LOG2E = math.log2(math.e)
MESH = pl.DeviceIdType.MESH
F32 = jnp.float32
BF16 = jnp.bfloat16


def gelu_tanh(values):
    half = 0.5 * values
    c0 = math.sqrt(2.0 / math.pi)
    return half * jnp.tanh(values * (c0 + (c0 * 0.044715) * (values * values))) + half


def make_tables(position_bias, shifted, table, head_mask):
    tokens = G * G
    side = 2 * G - 1
    reach = (G - 1) * side + G
    shifted[...] = jnp.zeros(shifted.shape, F32)
    for u in range(tokens):
        offset = (G - 1 - u // G) * side + (G - 1 - u % G)
        for h in range(HEADS):
            shifted[h * tokens + u : h * tokens + u + 1, :reach] = position_bias[
                h : h + 1, offset : offset + reach
            ]
    lane = lax.broadcasted_iota(jnp.int32, (128, 2 * tokens), 1) % tokens
    entry = lax.broadcasted_iota(jnp.int32, (128, 2 * tokens), 0)
    pick = (entry == (lane // G) * side + lane % G).astype(F32)
    table[...] = LOG2E * jnp.dot(
        shifted[...], pick, precision=lax.Precision.HIGHEST, preferred_element_type=F32
    )
    channels = head_mask.shape[1]
    of_row = lax.broadcasted_iota(jnp.int32, head_mask.shape, 0) // tokens
    of_lane = lax.broadcasted_iota(jnp.int32, head_mask.shape, 1) // (channels // HEADS)
    head_mask[...] = (of_row == of_lane).astype(F32).astype(BF16)


def kernel(
    sizes,
    sky,
    expand_weight,
    expand_bias,
    depth_weight,
    depth_bias,
    project_weight,
    project_bias,
    norm_gain,
    norm_bias,
    mixing_weight,
    position_bias,
    output_weight,
    out,
    halo_rows,
    halo_cols,
    expanded,
    side,
    t_left,
    t_mid,
    t_right,
    hidden,
    normed,
    received,
    group_in,
    group_out,
    attended,
    returned,
    halo_send,
    halo_recv,
    shifted,
    table,
    head_mask,
    forward_send,
    forward_recv,
    back_send,
    back_recv,
):
    row_size, col_size = sizes
    rows, cols, channels = sky.shape
    chunks = rows // G
    across = G // col_size
    stride = cols // across
    width = stride // col_size
    tokens = G * G
    slots = G * col_size
    repeat = row_size // G

    face = lax.axis_index("groups")
    row = lax.axis_index("row")
    col = lax.axis_index("col")
    other = 1 - col
    my_p = row // repeat
    parity = row % repeat
    me = my_p * col_size + col
    has_up = row > 0
    has_down = row < row_size - 1

    def partner(j):
        slot = (me + 8 + ((j + 1) // 2) * (2 * (j % 2) - 1)) % slots
        p, c = slot // col_size, slot % col_size
        return slot, p, c, (face, p * repeat + parity, c)

    barrier = pltpu.get_barrier_semaphore()

    def greet(j, carry):
        pl.semaphore_signal(barrier, inc=1, device_id=partner(j)[3], device_id_type=MESH)
        return carry

    lax.fori_loop(0, slots - 1, greet, 0)
    pl.semaphore_wait(barrier, slots - 1)
    if repeat > 1:
        for there, near in ((has_up, row - 1), (has_down, row + 1)):

            @pl.when(there)
            def _():
                for c in (col, other):
                    pl.semaphore_signal(barrier, inc=1, device_id=(face, near, c), device_id_type=MESH)

        for there in (has_up, has_down):

            @pl.when(there)
            def _():
                pl.semaphore_wait(barrier, 2)

    edge_start = pl.multiple_of(other * (cols - EDGE), EDGE)
    edge = pl.ds(edge_start, EDGE)

    def remote(src, dst, i, j, device):
        return pltpu.make_async_remote_copy(
            src_ref=src,
            dst_ref=dst,
            send_sem=halo_send.at[i],
            recv_sem=halo_recv.at[j],
            device_id=device,
            device_id_type=MESH,
        )

    up_row = remote(sky.at[0], halo_rows.at[1], 0, 1, (face, row - 1, col))
    up_corner = remote(sky.at[0, edge], halo_cols.at[rows + 1], 1, 4, (face, row - 1, other))
    down_row = remote(sky.at[rows - 1], halo_rows.at[0], 2, 0, (face, row + 1, col))
    down_corner = remote(sky.at[rows - 1, edge], halo_cols.at[0], 3, 3, (face, row + 1, other))
    side_copy = remote(sky.at[:, edge], halo_cols.at[pl.ds(1, rows)], 4, 2, (face, row, other))

    @pl.when(has_up)
    def _():
        up_row.start()
        up_corner.start()

    @pl.when(has_down)
    def _():
        down_row.start()
        down_corner.start()

    side_copy.start()

    def expand(features):
        return gelu_tanh(
            jnp.dot(features, expand_weight[...], preferred_element_type=F32) + expand_bias[...]
        ).astype(BF16)

    def put_row(i, values):
        expanded[0, i] = values[:, :128]
        expanded[1, i] = values[:, 128:]

    def expand_row(i):
        put_row(i + 1, expand(sky[i]))

    half = G // 2
    far = (my_p // half + 1) % 2 * half

    def target(j):
        return (far + (my_p + j) % half + (j // half) * half) % G

    def expand_first(j):
        i = target(j) * chunks
        expand_row(i)
        expand_row(i + 1)

        @pl.when(i > 0)
        def _():
            expand_row(i - 1)

    expand_first(0)

    side_copy.wait_recv()
    strip = expand(halo_cols[1 : rows + 1].reshape(rows * EDGE, channels)).astype(F32)
    side[0, 1 : rows + 1] = strip[:, :128].reshape(rows, EDGE, 128)
    side[1, 1 : rows + 1] = strip[:, 128:].reshape(rows, EDGE, 128)
    for there, slot, at, row_copy, corner_copy in (
        (has_up, 0, 0, down_row, down_corner),
        (has_down, 1, rows + 1, up_row, up_corner),
    ):

        @pl.when(there)
        def _():
            row_copy.wait_recv()
            corner_copy.wait_recv()
            put_row(at, expand(halo_rows[slot]))
            corner = expand(halo_cols[at]).astype(F32)
            side[0, at] = corner[:, :128]
            side[1, at] = corner[:, 128:]

        @pl.when(jnp.logical_not(there))
        def _():
            put_row(at, jnp.zeros((cols, 256), BF16))
            side[:, at] = jnp.zeros((2, EDGE, 128), F32)

    edge_at = other * 0 + col * (EDGE - 1)
    on_left = col.astype(F32)
    on_right = 1.0 - on_left
    tile = 128

    def conv_row(k, d):
        i = d * chunks + k
        for h in range(2):
            lanes = slice(h * 128, h * 128 + 128)
            taps = [[depth_weight[a, b : b + 1, lanes] for b in range(3)] for a in range(3)]
            for j in range(0, cols, tile):
                cells = [expanded[h, i + a, j : j + tile, :].astype(F32) for a in range(3)]
                for b, buffer in ((0, t_left), (1, t_mid), (2, t_right)):
                    buffer[h, 8 + j : 8 + j + tile] = (
                        cells[0] * taps[0][b] + cells[1] * taps[1][b] + cells[2] * taps[2][b]
                    )
            beyond = [side[h, i + a, pl.ds(edge_at, 1), :] for a in range(3)]
            for b, buffer, at, on in ((0, t_left, 7, on_left), (2, t_right, 8 + cols, on_right)):
                buffer[h, at : at + 1] = on * (
                    beyond[0] * taps[0][b] + beyond[1] * taps[1][b] + beyond[2] * taps[2][b]
                )
            for j in range(0, cols, tile):
                total = (
                    t_left[h, 7 + j : 7 + j + tile]
                    + t_mid[h, 8 + j : 8 + j + tile]
                    + t_right[h, 9 + j : 9 + j + tile]
                    + depth_bias[:, lanes]
                )
                hidden[j : j + tile, lanes] = gelu_tanh(total).astype(BF16)
        for j in range(0, cols, tile):
            after = (
                sky[i, j : j + tile].astype(F32)
                + jnp.dot(hidden[j : j + tile], project_weight[...], preferred_element_type=F32)
                + project_bias[...]
            ).astype(BF16)
            out[i, j : j + tile] = after
            values = after.astype(F32)
            centred = values - jnp.mean(values, axis=-1, keepdims=True)
            variance = jnp.mean(centred * centred, axis=-1, keepdims=True)
            normed[k, d, j // stride, j % stride : j % stride + tile] = (
                centred * lax.rsqrt(variance + 1e-05) * norm_gain[...] + norm_bias[...]
            ).astype(BF16)

    def forward_copy(k, p, c):
        return pltpu.make_async_remote_copy(
            src_ref=normed.at[k, p, :, pl.ds(c * width, width)],
            dst_ref=received.at[k, me],
            send_sem=forward_send.at[k],
            recv_sem=forward_recv.at[k],
            device_id=(face, p * repeat + parity, c),
            device_id_type=MESH,
        )

    my_cols = pl.ds(pl.multiple_of(col * width, width), width)

    def back_copy(k, j):
        slot, _, _, device = partner(j)
        return pltpu.make_async_remote_copy(
            src_ref=attended.at[k, slot],
            dst_ref=returned.at[k, my_p, :, my_cols],
            send_sem=back_send.at[k],
            recv_sem=back_recv.at[k],
            device_id=device,
            device_id_type=MESH,
        )

    def conv_step(s, carry):
        k, j = s // G, s % G
        d = target(j)

        @pl.when((k > 0) & (k < chunks - 2))
        def _():
            expand_row(d * chunks + k + 1)

        conv_row(k, d)
        for c in range(col_size):
            mine = (d == my_p) & (c == col)

            @pl.when(jnp.logical_not(mine))
            def _():
                forward_copy(k, d, c).start()

            @pl.when(mine)
            def _():
                pltpu.make_async_copy(
                    normed.at[k, my_p, :, my_cols], received.at[k, me], forward_recv.at[k]
                ).start()

        @pl.when((k == 0) & (j < G - 1))
        def _():
            expand_first(j + 1)

        @pl.when((k == 0) & (j == G - 1))
        def _():
            expand_row(rows - 1)

        return carry

    lax.fori_loop(0, chunks * G, conv_step, 0)

    scale = LOG2E / math.sqrt(channels // HEADS)
    make_tables(position_bias, shifted, table, head_mask)
    bundle = 8

    def attend_pair(first, second):
        keys, queries, values = [], [], []
        zero = jnp.zeros((tokens, channels), BF16)
        for projected in (first, second):
            key = projected[:, channels : 2 * channels]
            value = projected[:, 2 * channels :]
            keys.append(jnp.concatenate([key] * HEADS, axis=0) * head_mask[...])
            values.append(jnp.concatenate([value] * HEADS, axis=0) * head_mask[...])
        queries = jnp.concatenate(
            [
                jnp.concatenate([first[:, :channels], zero], axis=1),
                jnp.concatenate([zero, second[:, :channels]], axis=1),
            ],
            axis=0,
        )
        scores = lax.dot_general(
            jnp.concatenate(keys, axis=1),
            queries,
            (((1,), (1,)), ((), ())),
            preferred_element_type=F32,
        )
        scores = (scores * scale + table[...]).reshape(HEADS, tokens, 2 * tokens)
        powers = jnp.exp2(scores - jnp.max(scores, axis=1, keepdims=True))
        probs = powers * (1.0 / jnp.sum(powers, axis=1, keepdims=True))
        result = lax.dot_general(
            probs.astype(BF16).reshape(HEADS * tokens, 2 * tokens),
            jnp.concatenate(values, axis=1),
            (((0,), (0,)), ((), ())),
            preferred_element_type=F32,
        )
        return result[:tokens, :channels], result[tokens:, channels:]

    def attend_chunk(k, carry):
        pltpu.make_async_copy(received.at[k], received.at[k], forward_recv.at[k]).wait()

        def widen(s, inner):
            group_in[pl.ds(pl.multiple_of(s * across * width, across * width), across * width)] = (
                received[k, s].reshape(across * width, channels).astype(F32)
            )
            return inner

        lax.fori_loop(0, slots, widen, 0)

        def some_groups(b, inner):
            start = b * bundle
            features = jnp.concatenate(
                [group_in[pl.ds(start + n, tokens, stride=width), :] for n in range(bundle)], axis=0
            ).astype(BF16)
            projected = jnp.dot(features, mixing_weight[...], preferred_element_type=F32).astype(BF16)
            parts = [projected[n * tokens : (n + 1) * tokens] for n in range(bundle)]
            for n in range(0, bundle, 2):
                first, second = attend_pair(parts[n], parts[n + 1])
                group_out[pl.ds(start + n, tokens, stride=width), :] = first
                group_out[pl.ds(start + n + 1, tokens, stride=width), :] = second
            return inner

        lax.fori_loop(0, width // bundle, some_groups, 0)

        def narrow(s, inner):
            attended[k, s] = (
                group_out[pl.ds(pl.multiple_of(s * across * width, across * width), across * width)]
                .astype(BF16)
                .reshape(across, width, channels)
            )
            return inner

        lax.fori_loop(0, slots, narrow, 0)

        def send(j, inner):
            back_copy(k, j).start()
            return inner

        lax.fori_loop(0, slots - 1, send, 0)
        pltpu.make_async_copy(
            attended.at[k, me], returned.at[k, my_p, :, my_cols], back_recv.at[k]
        ).start()
        return carry

    lax.fori_loop(0, chunks, attend_chunk, 0)

    def finish_chunk(k, carry):
        pltpu.make_async_copy(returned.at[k], returned.at[k], back_recv.at[k]).wait()

        def one(d, inner):
            i = d * chunks + k
            out[i] = (
                out[i].astype(F32)
                + jnp.dot(
                    returned[k, d].reshape(cols, channels),
                    output_weight[...],
                    preferred_element_type=F32,
                )
            ).astype(BF16)
            return inner

        lax.fori_loop(0, G, one, 0)
        return carry

    lax.fori_loop(0, chunks, finish_chunk, 0)

    def drain(k, carry):
        sent = received.at[k, pl.ds(0, slots - 1)]
        pltpu.make_async_copy(sent, sent, forward_send.at[k]).wait()
        pltpu.make_async_copy(sent, sent, back_send.at[k]).wait()
        return carry

    lax.fori_loop(0, chunks, drain, 0)

    @pl.when(has_up)
    def _():
        up_row.wait_send()
        up_corner.wait_send()

    @pl.when(has_down)
    def _():
        down_row.wait_send()
        down_corner.wait_send()

    side_copy.wait_send()


def body(
    sizes,
    sky_map,
    expand_weight,
    expand_bias,
    depth_weight,
    depth_bias,
    project_weight,
    project_bias,
    norm_gain,
    norm_bias,
    mixing_weight,
    position_bias,
    output_weight,
):
    rows, cols, channels = sky_map.shape
    wide = expand_weight.shape[1]
    col_size = sizes[1]
    chunks = rows // G
    across = G // col_size
    stride = cols // across
    width = stride // col_size
    slots = G * col_size
    tokens = G * G
    vmem = pl.BlockSpec(memory_space=pltpu.VMEM)
    dma = pltpu.SemaphoreType.DMA
    return pl.pallas_call(
        functools.partial(kernel, sizes),
        out_shape=jax.ShapeDtypeStruct(sky_map.shape, BF16),
        in_specs=[vmem] * 12,
        out_specs=vmem,
        scratch_shapes=[
            pltpu.VMEM((2, cols, channels), BF16),
            pltpu.VMEM((rows + 2, EDGE, channels), BF16),
            pltpu.VMEM((2, rows + 2, cols, 128), BF16),
            pltpu.VMEM((2, rows + 2, EDGE, 128), F32),
            pltpu.VMEM((2, cols + 16, 128), F32),
            pltpu.VMEM((2, cols + 16, 128), F32),
            pltpu.VMEM((2, cols + 16, 128), F32),
            pltpu.VMEM((cols, wide), BF16),
            pltpu.VMEM((chunks, G, across, stride, channels), BF16),
            pltpu.VMEM((chunks, slots, across, width, channels), BF16),
            pltpu.VMEM((tokens * width, channels), F32),
            pltpu.VMEM((tokens * width, channels), F32),
            pltpu.VMEM((chunks, slots, across, width, channels), BF16),
            pltpu.VMEM((chunks, G, across, stride, channels), BF16),
            dma((5,)),
            dma((5,)),
            pltpu.VMEM((HEADS * tokens, 128), F32),
            pltpu.VMEM((HEADS * tokens, 2 * tokens), F32),
            pltpu.VMEM((HEADS * tokens, channels), BF16),
            dma((chunks,)),
            dma((chunks,)),
            dma((chunks,)),
            dma((chunks,)),
        ],
        compiler_params=pltpu.CompilerParams(
            collective_id=0, has_side_effects=True, vmem_limit_bytes=58 * 1024 * 1024
        ),
    )(
        sky_map,
        expand_weight,
        expand_bias.reshape(1, wide),
        depth_weight,
        depth_bias.reshape(1, wide),
        project_weight,
        project_bias.reshape(1, channels),
        norm_gain.reshape(1, channels),
        norm_bias.reshape(1, channels),
        mixing_weight,
        position_bias,
        output_weight,
    )


def solution(mesh):
    placed = (P(("groups", "row"), "col", None),) + (P(),) * 11
    sizes = (mesh.shape["row"], mesh.shape["col"])
    return jax.shard_map(
        functools.partial(body, sizes),
        mesh=mesh,
        in_specs=placed,
        out_specs=P(("groups", "row"), "col", None),
        check_vma=False,
    )
```

```python
import functools
import math

import jax
import jax.numpy as jnp
from jax import lax
from jax.experimental import pallas as pl
from jax.experimental.pallas import tpu as pltpu
from jax.sharding import PartitionSpec as P

HEADS = 4
G = 8
EDGE = 16
LOG2E = math.log2(math.e)
MESH = pl.DeviceIdType.MESH
F32 = jnp.float32
BF16 = jnp.bfloat16


def gelu_tanh(values):
    half = 0.5 * values
    c0 = math.sqrt(2.0 / math.pi)
    return half * jnp.tanh(values * (c0 + (c0 * 0.044715) * (values * values))) + half


def make_tables(position_bias, shifted, table, head_mask):
    tokens = G * G
    side = 2 * G - 1
    reach = (G - 1) * side + G
    shifted[...] = jnp.zeros(shifted.shape, F32)
    for u in range(tokens):
        offset = (G - 1 - u // G) * side + (G - 1 - u % G)
        for h in range(HEADS):
            shifted[h * tokens + u : h * tokens + u + 1, :reach] = position_bias[
                h : h + 1, offset : offset + reach
            ]
    lane = lax.broadcasted_iota(jnp.int32, (128, 2 * tokens), 1) % tokens
    entry = lax.broadcasted_iota(jnp.int32, (128, 2 * tokens), 0)
    pick = (entry == (lane // G) * side + lane % G).astype(F32)
    table[...] = LOG2E * jnp.dot(
        shifted[...], pick, precision=lax.Precision.HIGHEST, preferred_element_type=F32
    )
    channels = head_mask.shape[1]
    of_row = lax.broadcasted_iota(jnp.int32, head_mask.shape, 0) // tokens
    of_lane = lax.broadcasted_iota(jnp.int32, head_mask.shape, 1) // (channels // HEADS)
    head_mask[...] = (of_row == of_lane).astype(F32).astype(BF16)


def kernel(
    sizes,
    sky_map,
    expand_weight,
    expand_bias,
    depth_weight,
    depth_bias,
    project_weight,
    project_bias,
    norm_gain,
    norm_bias,
    mixing_weight,
    position_bias,
    output_weight,
    block_out,
    sky,
    out,
    halo_rows,
    halo_cols,
    expanded,
    side,
    t_left,
    t_mid,
    t_right,
    hidden,
    normed,
    received,
    group_in,
    group_out,
    attended,
    returned,
    halo_send,
    halo_recv,
    shifted,
    table,
    head_mask,
    forward_send,
    forward_recv,
    back_send,
    back_recv,
    load_sem,
    store_sem,
):
    row_size, col_size = sizes
    rows, cols, channels = sky.shape
    chunks = rows // G
    across = G // col_size
    stride = cols // across
    width = stride // col_size
    tokens = G * G
    slots = G * col_size
    repeat = row_size // G

    face = lax.axis_index("groups")
    row = lax.axis_index("row")
    col = lax.axis_index("col")
    other = 1 - col
    my_p = row // repeat
    parity = row % repeat
    me = my_p * col_size + col
    has_up = row > 0
    has_down = row < row_size - 1

    def partner(j):
        slot = (me + 8 + ((j + 1) // 2) * (2 * (j % 2) - 1)) % slots
        p, c = slot // col_size, slot % col_size
        return slot, p, c, (face, p * repeat + parity, c)

    part = rows // load_sem.shape[0]
    loads = [
        pltpu.make_async_copy(
            sky_map.at[pl.ds(n * part, part)], sky.at[pl.ds(n * part, part)], load_sem.at[n]
        )
        for n in range(load_sem.shape[0])
    ]
    for load in loads:
        load.start()
    barrier = pltpu.get_barrier_semaphore()

    def greet(j, carry):
        pl.semaphore_signal(barrier, inc=1, device_id=partner(j)[3], device_id_type=MESH)
        return carry

    lax.fori_loop(0, slots - 1, greet, 0)
    pl.semaphore_wait(barrier, slots - 1)
    if repeat > 1:
        for there, near in ((has_up, row - 1), (has_down, row + 1)):

            @pl.when(there)
            def _():
                for c in (col, other):
                    pl.semaphore_signal(barrier, inc=1, device_id=(face, near, c), device_id_type=MESH)

        for there in (has_up, has_down):

            @pl.when(there)
            def _():
                pl.semaphore_wait(barrier, 2)

    edge_start = pl.multiple_of(other * (cols - EDGE), EDGE)
    edge = pl.ds(edge_start, EDGE)

    def remote(src, dst, i, j, device):
        return pltpu.make_async_remote_copy(
            src_ref=src,
            dst_ref=dst,
            send_sem=halo_send.at[i],
            recv_sem=halo_recv.at[j],
            device_id=device,
            device_id_type=MESH,
        )

    up_row = remote(sky_map.at[0], halo_rows.at[1], 0, 1, (face, row - 1, col))
    up_corner = remote(sky_map.at[0, edge], halo_cols.at[rows + 1], 1, 4, (face, row - 1, other))
    down_row = remote(sky_map.at[rows - 1], halo_rows.at[0], 2, 0, (face, row + 1, col))
    down_corner = remote(sky_map.at[rows - 1, edge], halo_cols.at[0], 3, 3, (face, row + 1, other))
    side_copy = remote(sky_map.at[:, edge], halo_cols.at[pl.ds(1, rows)], 4, 2, (face, row, other))

    @pl.when(has_up)
    def _():
        up_row.start()
        up_corner.start()

    @pl.when(has_down)
    def _():
        down_row.start()
        down_corner.start()

    side_copy.start()

    def expand(features):
        return gelu_tanh(
            jnp.dot(features, expand_weight[...], preferred_element_type=F32) + expand_bias[...]
        ).astype(BF16)

    def put_row(i, values):
        expanded[0, i] = values[:, :128]
        expanded[1, i] = values[:, 128:]

    def expand_row(i):
        put_row(i + 1, expand(sky[i]))

    half = G // 2
    far = (my_p // half + 1) % 2 * half

    def target(j):
        return (far + (my_p + j) % half + (j // half) * half) % G

    def expand_first(j):
        i = target(j) * chunks
        expand_row(i)
        expand_row(i + 1)

        @pl.when(i > 0)
        def _():
            expand_row(i - 1)

    for load in loads:
        load.wait()
    expand_first(0)

    side_copy.wait_recv()
    strip = expand(halo_cols[1 : rows + 1].reshape(rows * EDGE, channels)).astype(F32)
    side[0, 1 : rows + 1] = strip[:, :128].reshape(rows, EDGE, 128)
    side[1, 1 : rows + 1] = strip[:, 128:].reshape(rows, EDGE, 128)
    for there, slot, at, row_copy, corner_copy in (
        (has_up, 0, 0, down_row, down_corner),
        (has_down, 1, rows + 1, up_row, up_corner),
    ):

        @pl.when(there)
        def _():
            row_copy.wait_recv()
            corner_copy.wait_recv()
            put_row(at, expand(halo_rows[slot]))
            corner = expand(halo_cols[at]).astype(F32)
            side[0, at] = corner[:, :128]
            side[1, at] = corner[:, 128:]

        @pl.when(jnp.logical_not(there))
        def _():
            put_row(at, jnp.zeros((cols, 256), BF16))
            side[:, at] = jnp.zeros((2, EDGE, 128), F32)

    edge_at = other * 0 + col * (EDGE - 1)
    on_left = col.astype(F32)
    on_right = 1.0 - on_left
    tile = 128

    def conv_row(k, d):
        i = d * chunks + k
        for h in range(2):
            lanes = slice(h * 128, h * 128 + 128)
            taps = [[depth_weight[a, b : b + 1, lanes] for b in range(3)] for a in range(3)]
            for j in range(0, cols, tile):
                cells = [expanded[h, i + a, j : j + tile, :].astype(F32) for a in range(3)]
                for b, buffer in ((0, t_left), (1, t_mid), (2, t_right)):
                    buffer[h, 8 + j : 8 + j + tile] = (
                        cells[0] * taps[0][b] + cells[1] * taps[1][b] + cells[2] * taps[2][b]
                    )
            beyond = [side[h, i + a, pl.ds(edge_at, 1), :] for a in range(3)]
            for b, buffer, at, on in ((0, t_left, 7, on_left), (2, t_right, 8 + cols, on_right)):
                buffer[h, at : at + 1] = on * (
                    beyond[0] * taps[0][b] + beyond[1] * taps[1][b] + beyond[2] * taps[2][b]
                )
            for j in range(0, cols, tile):
                total = (
                    t_left[h, 7 + j : 7 + j + tile]
                    + t_mid[h, 8 + j : 8 + j + tile]
                    + t_right[h, 9 + j : 9 + j + tile]
                    + depth_bias[:, lanes]
                )
                hidden[j : j + tile, lanes] = gelu_tanh(total).astype(BF16)
        for j in range(0, cols, tile):
            after = (
                sky[i, j : j + tile].astype(F32)
                + jnp.dot(hidden[j : j + tile], project_weight[...], preferred_element_type=F32)
                + project_bias[...]
            ).astype(BF16)
            out[i, j : j + tile] = after
            values = after.astype(F32)
            centred = values - jnp.mean(values, axis=-1, keepdims=True)
            variance = jnp.mean(centred * centred, axis=-1, keepdims=True)
            normed[k, d, j // stride, j % stride : j % stride + tile] = (
                centred * lax.rsqrt(variance + 1e-05) * norm_gain[...] + norm_bias[...]
            ).astype(BF16)

    def forward_copy(k, p, c):
        return pltpu.make_async_remote_copy(
            src_ref=normed.at[k, p, :, pl.ds(c * width, width)],
            dst_ref=received.at[k, me],
            send_sem=forward_send.at[k],
            recv_sem=forward_recv.at[k],
            device_id=(face, p * repeat + parity, c),
            device_id_type=MESH,
        )

    my_cols = pl.ds(pl.multiple_of(col * width, width), width)

    def back_copy(k, j):
        slot, _, _, device = partner(j)
        return pltpu.make_async_remote_copy(
            src_ref=attended.at[k, slot],
            dst_ref=returned.at[k, my_p, :, my_cols],
            send_sem=back_send.at[k],
            recv_sem=back_recv.at[k],
            device_id=device,
            device_id_type=MESH,
        )

    def conv_step(s, carry):
        k, j = s // G, s % G
        d = target(j)

        @pl.when((k > 0) & (k < chunks - 2))
        def _():
            expand_row(d * chunks + k + 1)

        conv_row(k, d)
        for c in range(col_size):
            mine = (d == my_p) & (c == col)

            @pl.when(jnp.logical_not(mine))
            def _():
                forward_copy(k, d, c).start()

            @pl.when(mine)
            def _():
                pltpu.make_async_copy(
                    normed.at[k, my_p, :, my_cols], received.at[k, me], forward_recv.at[k]
                ).start()

        @pl.when((k == 0) & (j < G - 1))
        def _():
            expand_first(j + 1)

        @pl.when((k == 0) & (j == G - 1))
        def _():
            expand_row(rows - 1)

        return carry

    lax.fori_loop(0, chunks * G, conv_step, 0)

    scale = LOG2E / math.sqrt(channels // HEADS)
    make_tables(position_bias, shifted, table, head_mask)
    bundle = 8

    def attend_pair(first, second):
        keys, queries, values = [], [], []
        zero = jnp.zeros((tokens, channels), BF16)
        for projected in (first, second):
            key = projected[:, channels : 2 * channels]
            value = projected[:, 2 * channels :]
            keys.append(jnp.concatenate([key] * HEADS, axis=0) * head_mask[...])
            values.append(jnp.concatenate([value] * HEADS, axis=0) * head_mask[...])
        queries = jnp.concatenate(
            [
                jnp.concatenate([first[:, :channels], zero], axis=1),
                jnp.concatenate([zero, second[:, :channels]], axis=1),
            ],
            axis=0,
        )
        scores = lax.dot_general(
            jnp.concatenate(keys, axis=1),
            queries,
            (((1,), (1,)), ((), ())),
            preferred_element_type=F32,
        )
        scores = (scores * scale + table[...]).reshape(HEADS, tokens, 2 * tokens)
        powers = jnp.exp2(scores - jnp.max(scores, axis=1, keepdims=True))
        probs = powers * (1.0 / jnp.sum(powers, axis=1, keepdims=True))
        result = lax.dot_general(
            probs.astype(BF16).reshape(HEADS * tokens, 2 * tokens),
            jnp.concatenate(values, axis=1),
            (((0,), (0,)), ((), ())),
            preferred_element_type=F32,
        )
        return result[:tokens, :channels], result[tokens:, channels:]

    def attend_chunk(k, carry):
        pltpu.make_async_copy(received.at[k], received.at[k], forward_recv.at[k]).wait()

        def widen(s, inner):
            group_in[pl.ds(pl.multiple_of(s * across * width, across * width), across * width)] = (
                received[k, s].reshape(across * width, channels).astype(F32)
            )
            return inner

        lax.fori_loop(0, slots, widen, 0)

        def some_groups(b, inner):
            start = b * bundle
            features = jnp.concatenate(
                [group_in[pl.ds(start + n, tokens, stride=width), :] for n in range(bundle)], axis=0
            ).astype(BF16)
            projected = jnp.dot(features, mixing_weight[...], preferred_element_type=F32).astype(BF16)
            parts = [projected[n * tokens : (n + 1) * tokens] for n in range(bundle)]
            for n in range(0, bundle, 2):
                first, second = attend_pair(parts[n], parts[n + 1])
                group_out[pl.ds(start + n, tokens, stride=width), :] = first
                group_out[pl.ds(start + n + 1, tokens, stride=width), :] = second
            return inner

        lax.fori_loop(0, width // bundle, some_groups, 0)

        def narrow(s, inner):
            attended[k, s] = (
                group_out[pl.ds(pl.multiple_of(s * across * width, across * width), across * width)]
                .astype(BF16)
                .reshape(across, width, channels)
            )
            return inner

        lax.fori_loop(0, slots, narrow, 0)

        def send(j, inner):
            back_copy(k, j).start()
            return inner

        lax.fori_loop(0, slots - 1, send, 0)
        pltpu.make_async_copy(
            attended.at[k, me], returned.at[k, my_p, :, my_cols], back_recv.at[k]
        ).start()
        return carry

    lax.fori_loop(0, chunks, attend_chunk, 0)

    def finish_chunk(k, carry):
        pltpu.make_async_copy(returned.at[k], returned.at[k], back_recv.at[k]).wait()

        def one(d, inner):
            i = d * chunks + k
            out[i] = (
                out[i].astype(F32)
                + jnp.dot(
                    returned[k, d].reshape(cols, channels),
                    output_weight[...],
                    preferred_element_type=F32,
                )
            ).astype(BF16)
            pltpu.make_async_copy(out.at[i], block_out.at[i], store_sem.at[k]).start()
            return inner

        lax.fori_loop(0, G, one, 0)
        return carry

    lax.fori_loop(0, chunks, finish_chunk, 0)

    def drain(k, carry):
        sent = received.at[k, pl.ds(0, slots - 1)]
        pltpu.make_async_copy(sent, sent, forward_send.at[k]).wait()
        pltpu.make_async_copy(sent, sent, back_send.at[k]).wait()
        stored = out.at[pl.ds(0, G)]
        pltpu.make_async_copy(stored, stored, store_sem.at[k]).wait()
        return carry

    lax.fori_loop(0, chunks, drain, 0)

    @pl.when(has_up)
    def _():
        up_row.wait_send()
        up_corner.wait_send()

    @pl.when(has_down)
    def _():
        down_row.wait_send()
        down_corner.wait_send()

    side_copy.wait_send()


def body(
    sizes,
    sky_map,
    expand_weight,
    expand_bias,
    depth_weight,
    depth_bias,
    project_weight,
    project_bias,
    norm_gain,
    norm_bias,
    mixing_weight,
    position_bias,
    output_weight,
):
    rows, cols, channels = sky_map.shape
    wide = expand_weight.shape[1]
    col_size = sizes[1]
    chunks = rows // G
    across = G // col_size
    stride = cols // across
    width = stride // col_size
    slots = G * col_size
    tokens = G * G
    vmem = pl.BlockSpec(memory_space=pltpu.VMEM)
    anywhere = pl.BlockSpec(memory_space=pl.ANY)
    dma = pltpu.SemaphoreType.DMA
    return pl.pallas_call(
        functools.partial(kernel, sizes),
        out_shape=jax.ShapeDtypeStruct(sky_map.shape, BF16),
        in_specs=[anywhere] + [vmem] * 11,
        out_specs=anywhere,
        scratch_shapes=[
            pltpu.VMEM(sky_map.shape, BF16),
            pltpu.VMEM(sky_map.shape, BF16),
            pltpu.VMEM((2, cols, channels), BF16),
            pltpu.VMEM((rows + 2, EDGE, channels), BF16),
            pltpu.VMEM((2, rows + 2, cols, 128), BF16),
            pltpu.VMEM((2, rows + 2, EDGE, 128), F32),
            pltpu.VMEM((2, cols + 16, 128), F32),
            pltpu.VMEM((2, cols + 16, 128), F32),
            pltpu.VMEM((2, cols + 16, 128), F32),
            pltpu.VMEM((cols, wide), BF16),
            pltpu.VMEM((chunks, G, across, stride, channels), BF16),
            pltpu.VMEM((chunks, slots, across, width, channels), BF16),
            pltpu.VMEM((tokens * width, channels), F32),
            pltpu.VMEM((tokens * width, channels), F32),
            pltpu.VMEM((chunks, slots, across, width, channels), BF16),
            pltpu.VMEM((chunks, G, across, stride, channels), BF16),
            dma((5,)),
            dma((5,)),
            pltpu.VMEM((HEADS * tokens, 128), F32),
            pltpu.VMEM((HEADS * tokens, 2 * tokens), F32),
            pltpu.VMEM((HEADS * tokens, channels), BF16),
            dma((chunks,)),
            dma((chunks,)),
            dma((chunks,)),
            dma((chunks,)),
            dma((4,)),
            dma((chunks,)),
        ],
        compiler_params=pltpu.CompilerParams(
            collective_id=0, has_side_effects=True, vmem_limit_bytes=58 * 1024 * 1024
        ),
    )(
        sky_map,
        expand_weight,
        expand_bias.reshape(1, wide),
        depth_weight,
        depth_bias.reshape(1, wide),
        project_weight,
        project_bias.reshape(1, channels),
        norm_gain.reshape(1, channels),
        norm_bias.reshape(1, channels),
        mixing_weight,
        position_bias,
        output_weight,
    )


def solution(mesh):
    placed = (P(("groups", "row"), "col", None),) + (P(),) * 11
    sizes = (mesh.shape["row"], mesh.shape["col"])
    return jax.shard_map(
        functools.partial(body, sizes),
        mesh=mesh,
        in_specs=placed,
        out_specs=P(("groups", "row"), "col", None),
        check_vma=False,
    )
```

```python
import functools
import math

import jax
import jax.numpy as jnp
from jax import lax
from jax.experimental import pallas as pl
from jax.experimental.pallas import tpu as pltpu
from jax.sharding import PartitionSpec as P

HEADS = 4
G = 8
EDGE = 16
LOG2E = math.log2(math.e)
MESH = pl.DeviceIdType.MESH
F32 = jnp.float32
BF16 = jnp.bfloat16


def gelu_tanh(values):
    half = 0.5 * values
    c0 = math.sqrt(2.0 / math.pi)
    return half * jnp.tanh(values * (c0 + (c0 * 0.044715) * (values * values))) + half


def make_tables(position_bias, shifted, table, head_mask):
    tokens = G * G
    side = 2 * G - 1
    reach = (G - 1) * side + G
    shifted[...] = jnp.zeros(shifted.shape, F32)
    for u in range(tokens):
        offset = (G - 1 - u // G) * side + (G - 1 - u % G)
        for h in range(HEADS):
            shifted[h * tokens + u : h * tokens + u + 1, :reach] = position_bias[
                h : h + 1, offset : offset + reach
            ]
    lane = lax.broadcasted_iota(jnp.int32, (128, 2 * tokens), 1) % tokens
    entry = lax.broadcasted_iota(jnp.int32, (128, 2 * tokens), 0)
    pick = (entry == (lane // G) * side + lane % G).astype(F32)
    table[...] = LOG2E * jnp.dot(
        shifted[...], pick, precision=lax.Precision.HIGHEST, preferred_element_type=F32
    )
    channels = head_mask.shape[1]
    of_row = lax.broadcasted_iota(jnp.int32, head_mask.shape, 0) // tokens
    of_lane = lax.broadcasted_iota(jnp.int32, head_mask.shape, 1) // (channels // HEADS)
    head_mask[...] = (of_row == of_lane).astype(F32).astype(BF16)


def kernel(
    sizes,
    sky_map,
    expand_weight,
    expand_bias,
    depth_weight,
    depth_bias,
    project_weight,
    project_bias,
    norm_gain,
    norm_bias,
    mixing_weight,
    position_bias,
    output_weight,
    block_out,
    sky,
    out,
    halo_rows,
    halo_cols,
    expanded,
    side,
    t_left,
    t_mid,
    t_right,
    hidden,
    normed,
    received,
    group_in,
    group_out,
    attended,
    returned,
    halo_send,
    halo_recv,
    shifted,
    table,
    head_mask,
    forward_send,
    forward_recv,
    back_send,
    back_recv,
    load_sem,
    store_sem,
):
    row_size, col_size = sizes
    rows, cols, channels = sky.shape
    chunks = rows // G
    across = G // col_size
    stride = cols // across
    width = stride // col_size
    tokens = G * G
    slots = G * col_size
    repeat = row_size // G

    face = lax.axis_index("groups")
    row = lax.axis_index("row")
    col = lax.axis_index("col")
    other = 1 - col
    my_p = row // repeat
    parity = row % repeat
    me = my_p * col_size + col
    has_up = row > 0
    has_down = row < row_size - 1

    def partner(j):
        slot = (me + 8 + ((j + 1) // 2) * (2 * (j % 2) - 1)) % slots
        p, c = slot // col_size, slot % col_size
        return slot, p, c, (face, p * repeat + parity, c)

    part = rows // load_sem.shape[0]
    loads = [
        pltpu.make_async_copy(
            sky_map.at[pl.ds(n * part, part)], sky.at[pl.ds(n * part, part)], load_sem.at[n]
        )
        for n in range(load_sem.shape[0])
    ]
    for load in loads:
        load.start()
    barrier = pltpu.get_barrier_semaphore()

    def greet(j, carry):
        pl.semaphore_signal(barrier, inc=1, device_id=partner(j)[3], device_id_type=MESH)
        return carry

    lax.fori_loop(0, slots - 1, greet, 0)
    pl.semaphore_wait(barrier, slots - 1)
    if repeat > 1:
        for there, near in ((has_up, row - 1), (has_down, row + 1)):

            @pl.when(there)
            def _():
                for c in (col, other):
                    pl.semaphore_signal(barrier, inc=1, device_id=(face, near, c), device_id_type=MESH)

        for there in (has_up, has_down):

            @pl.when(there)
            def _():
                pl.semaphore_wait(barrier, 2)

    edge_start = pl.multiple_of(other * (cols - EDGE), EDGE)
    edge = pl.ds(edge_start, EDGE)

    def remote(src, dst, i, j, device):
        return pltpu.make_async_remote_copy(
            src_ref=src,
            dst_ref=dst,
            send_sem=halo_send.at[i],
            recv_sem=halo_recv.at[j],
            device_id=device,
            device_id_type=MESH,
        )

    up_row = remote(sky_map.at[0], halo_rows.at[1], 0, 1, (face, row - 1, col))
    up_corner = remote(sky_map.at[0, edge], halo_cols.at[rows + 1], 1, 4, (face, row - 1, other))
    down_row = remote(sky_map.at[rows - 1], halo_rows.at[0], 2, 0, (face, row + 1, col))
    down_corner = remote(sky_map.at[rows - 1, edge], halo_cols.at[0], 3, 3, (face, row + 1, other))
    side_copy = remote(sky_map.at[:, edge], halo_cols.at[pl.ds(1, rows)], 4, 2, (face, row, other))

    @pl.when(has_up)
    def _():
        up_row.start()
        up_corner.start()

    @pl.when(has_down)
    def _():
        down_row.start()
        down_corner.start()

    side_copy.start()

    def expand(features):
        return gelu_tanh(
            jnp.dot(features, expand_weight[...], preferred_element_type=F32) + expand_bias[...]
        ).astype(BF16)

    def put_row(i, values):
        expanded[0, i] = values[:, :128]
        expanded[1, i] = values[:, 128:]

    def expand_row(i):
        put_row(i + 1, expand(sky[i]))

    half = G // 2
    far = (my_p // half + 1) % 2 * half

    def target(j):
        return (far + (my_p + j) % half + (j // half) * half) % G

    def expand_first(j):
        i = target(j) * chunks
        expand_row(i)
        expand_row(i + 1)

        @pl.when(i > 0)
        def _():
            expand_row(i - 1)

    for load in loads:
        load.wait()
    expand_first(0)

    side_copy.wait_recv()
    strip = expand(halo_cols[1 : rows + 1].reshape(rows * EDGE, channels)).astype(F32)
    side[0, 1 : rows + 1] = strip[:, :128].reshape(rows, EDGE, 128)
    side[1, 1 : rows + 1] = strip[:, 128:].reshape(rows, EDGE, 128)
    for there, slot, at, row_copy, corner_copy in (
        (has_up, 0, 0, down_row, down_corner),
        (has_down, 1, rows + 1, up_row, up_corner),
    ):

        @pl.when(there)
        def _():
            row_copy.wait_recv()
            corner_copy.wait_recv()
            put_row(at, expand(halo_rows[slot]))
            corner = expand(halo_cols[at]).astype(F32)
            side[0, at] = corner[:, :128]
            side[1, at] = corner[:, 128:]

        @pl.when(jnp.logical_not(there))
        def _():
            put_row(at, jnp.zeros((cols, 256), BF16))
            side[:, at] = jnp.zeros((2, EDGE, 128), F32)

    edge_at = other * 0 + col * (EDGE - 1)
    on_left = col.astype(F32)
    on_right = 1.0 - on_left
    tile = 128

    def conv_row(k, d):
        i = d * chunks + k
        for h in range(2):
            lanes = slice(h * 128, h * 128 + 128)
            taps = [[depth_weight[a, b : b + 1, lanes] for b in range(3)] for a in range(3)]
            for j in range(0, cols, tile):
                cells = [expanded[h, i + a, j : j + tile, :].astype(F32) for a in range(3)]
                for b, buffer in ((0, t_left), (1, t_mid), (2, t_right)):
                    buffer[h, 8 + j : 8 + j + tile] = (
                        cells[0] * taps[0][b] + cells[1] * taps[1][b] + cells[2] * taps[2][b]
                    )
            beyond = [side[h, i + a, pl.ds(edge_at, 1), :] for a in range(3)]
            for b, buffer, at, on in ((0, t_left, 7, on_left), (2, t_right, 8 + cols, on_right)):
                buffer[h, at : at + 1] = on * (
                    beyond[0] * taps[0][b] + beyond[1] * taps[1][b] + beyond[2] * taps[2][b]
                )
            for j in range(0, cols, tile):
                total = (
                    t_left[h, 7 + j : 7 + j + tile]
                    + t_mid[h, 8 + j : 8 + j + tile]
                    + t_right[h, 9 + j : 9 + j + tile]
                    + depth_bias[:, lanes]
                )
                hidden[j : j + tile, lanes] = gelu_tanh(total).astype(BF16)
        for j in range(0, cols, tile):
            after = (
                sky[i, j : j + tile].astype(F32)
                + jnp.dot(hidden[j : j + tile], project_weight[...], preferred_element_type=F32)
                + project_bias[...]
            ).astype(BF16)
            out[i, j : j + tile] = after
            values = after.astype(F32)
            centred = values - jnp.mean(values, axis=-1, keepdims=True)
            variance = jnp.mean(centred * centred, axis=-1, keepdims=True)
            normed[k, d, j // stride, j % stride : j % stride + tile] = (
                centred * lax.rsqrt(variance + 1e-05) * norm_gain[...] + norm_bias[...]
            ).astype(BF16)

    def forward_copy(k, p, c):
        return pltpu.make_async_remote_copy(
            src_ref=normed.at[k, p, :, pl.ds(c * width, width)],
            dst_ref=received.at[k, me],
            send_sem=forward_send.at[k],
            recv_sem=forward_recv.at[k],
            device_id=(face, p * repeat + parity, c),
            device_id_type=MESH,
        )

    my_cols = pl.ds(pl.multiple_of(col * width, width), width)

    def back_copy(k, p, c):
        slot = p * col_size + c
        device = (face, p * repeat + parity, c)
        return pltpu.make_async_remote_copy(
            src_ref=attended.at[k, slot],
            dst_ref=returned.at[k, my_p, :, my_cols],
            send_sem=back_send.at[k],
            recv_sem=back_recv.at[k],
            device_id=device,
            device_id_type=MESH,
        )

    def conv_step(s, carry):
        k, j = s // G, s % G
        d = target(j)

        @pl.when((k > 0) & (k < chunks - 2))
        def _():
            expand_row(d * chunks + k + 1)

        conv_row(k, d)
        for c in range(col_size):
            mine = (d == my_p) & (c == col)

            @pl.when(jnp.logical_not(mine))
            def _():
                forward_copy(k, d, c).start()

            @pl.when(mine)
            def _():
                pltpu.make_async_copy(
                    normed.at[k, my_p, :, my_cols], received.at[k, me], forward_recv.at[k]
                ).start()

        @pl.when((k == 0) & (j < G - 1))
        def _():
            expand_first(j + 1)

        @pl.when((k == 0) & (j == G - 1))
        def _():
            expand_row(rows - 1)

        return carry

    lax.fori_loop(0, chunks * G, conv_step, 0)

    scale = LOG2E / math.sqrt(channels // HEADS)
    make_tables(position_bias, shifted, table, head_mask)
    bundle = 8

    def attend_pair(first, second):
        keys, queries, values = [], [], []
        zero = jnp.zeros((tokens, channels), BF16)
        for projected in (first, second):
            key = projected[:, channels : 2 * channels]
            value = projected[:, 2 * channels :]
            keys.append(jnp.concatenate([key] * HEADS, axis=0) * head_mask[...])
            values.append(jnp.concatenate([value] * HEADS, axis=0) * head_mask[...])
        queries = jnp.concatenate(
            [
                jnp.concatenate([first[:, :channels], zero], axis=1),
                jnp.concatenate([zero, second[:, :channels]], axis=1),
            ],
            axis=0,
        )
        scores = lax.dot_general(
            jnp.concatenate(keys, axis=1),
            queries,
            (((1,), (1,)), ((), ())),
            preferred_element_type=F32,
        )
        scores = (scores * scale + table[...]).reshape(HEADS, tokens, 2 * tokens)
        powers = jnp.exp2(scores - jnp.max(scores, axis=1, keepdims=True))
        probs = powers * (1.0 / jnp.sum(powers, axis=1, keepdims=True))
        result = lax.dot_general(
            probs.astype(BF16).reshape(HEADS * tokens, 2 * tokens),
            jnp.concatenate(values, axis=1),
            (((0,), (0,)), ((), ())),
            preferred_element_type=F32,
        )
        return result[:tokens, :channels], result[tokens:, channels:]

    def attend_chunk(k, carry):
        pltpu.make_async_copy(received.at[k], received.at[k], forward_recv.at[k]).wait()

        def widen(s, inner):
            group_in[pl.ds(pl.multiple_of(s * across * width, across * width), across * width)] = (
                received[k, s].reshape(across * width, channels).astype(F32)
            )
            return inner

        lax.fori_loop(0, slots, widen, 0)

        def some_groups(b, inner):
            start = b * bundle
            features = jnp.concatenate(
                [group_in[pl.ds(start + n, tokens, stride=width), :] for n in range(bundle)], axis=0
            ).astype(BF16)
            projected = jnp.dot(features, mixing_weight[...], preferred_element_type=F32).astype(BF16)
            parts = [projected[n * tokens : (n + 1) * tokens] for n in range(bundle)]
            for n in range(0, bundle, 2):
                first, second = attend_pair(parts[n], parts[n + 1])
                group_out[pl.ds(start + n, tokens, stride=width), :] = first
                group_out[pl.ds(start + n + 1, tokens, stride=width), :] = second
            return inner

        lax.fori_loop(0, width // bundle, some_groups, 0)

        def narrow(s, inner):
            attended[k, s] = (
                group_out[pl.ds(pl.multiple_of(s * across * width, across * width), across * width)]
                .astype(BF16)
                .reshape(across, width, channels)
            )
            return inner

        lax.fori_loop(0, slots, narrow, 0)

        def send(j, inner):
            p = target(j)
            for c in range(col_size):

                @pl.when(jnp.logical_not((p == my_p) & (c == col)))
                def _():
                    back_copy(k, p, c).start()

            return inner

        lax.fori_loop(0, G, send, 0)
        pltpu.make_async_copy(
            attended.at[k, me], returned.at[k, my_p, :, my_cols], back_recv.at[k]
        ).start()
        return carry

    lax.fori_loop(0, chunks, attend_chunk, 0)

    def finish_chunk(k, carry):
        pltpu.make_async_copy(returned.at[k], returned.at[k], back_recv.at[k]).wait()

        def one(d, inner):
            i = d * chunks + k
            out[i] = (
                out[i].astype(F32)
                + jnp.dot(
                    returned[k, d].reshape(cols, channels),
                    output_weight[...],
                    preferred_element_type=F32,
                )
            ).astype(BF16)
            pltpu.make_async_copy(out.at[i], block_out.at[i], store_sem.at[k]).start()
            return inner

        lax.fori_loop(0, G, one, 0)
        return carry

    lax.fori_loop(0, chunks, finish_chunk, 0)

    def drain(k, carry):
        sent = received.at[k, pl.ds(0, slots - 1)]
        pltpu.make_async_copy(sent, sent, forward_send.at[k]).wait()
        pltpu.make_async_copy(sent, sent, back_send.at[k]).wait()
        stored = out.at[pl.ds(0, G)]
        pltpu.make_async_copy(stored, stored, store_sem.at[k]).wait()
        return carry

    lax.fori_loop(0, chunks, drain, 0)

    @pl.when(has_up)
    def _():
        up_row.wait_send()
        up_corner.wait_send()

    @pl.when(has_down)
    def _():
        down_row.wait_send()
        down_corner.wait_send()

    side_copy.wait_send()


def body(
    sizes,
    sky_map,
    expand_weight,
    expand_bias,
    depth_weight,
    depth_bias,
    project_weight,
    project_bias,
    norm_gain,
    norm_bias,
    mixing_weight,
    position_bias,
    output_weight,
):
    rows, cols, channels = sky_map.shape
    wide = expand_weight.shape[1]
    col_size = sizes[1]
    chunks = rows // G
    across = G // col_size
    stride = cols // across
    width = stride // col_size
    slots = G * col_size
    tokens = G * G
    vmem = pl.BlockSpec(memory_space=pltpu.VMEM)
    anywhere = pl.BlockSpec(memory_space=pl.ANY)
    dma = pltpu.SemaphoreType.DMA
    return pl.pallas_call(
        functools.partial(kernel, sizes),
        out_shape=jax.ShapeDtypeStruct(sky_map.shape, BF16),
        in_specs=[anywhere] + [vmem] * 11,
        out_specs=anywhere,
        scratch_shapes=[
            pltpu.VMEM(sky_map.shape, BF16),
            pltpu.VMEM(sky_map.shape, BF16),
            pltpu.VMEM((2, cols, channels), BF16),
            pltpu.VMEM((rows + 2, EDGE, channels), BF16),
            pltpu.VMEM((2, rows + 2, cols, 128), BF16),
            pltpu.VMEM((2, rows + 2, EDGE, 128), F32),
            pltpu.VMEM((2, cols + 16, 128), F32),
            pltpu.VMEM((2, cols + 16, 128), F32),
            pltpu.VMEM((2, cols + 16, 128), F32),
            pltpu.VMEM((cols, wide), BF16),
            pltpu.VMEM((chunks, G, across, stride, channels), BF16),
            pltpu.VMEM((chunks, slots, across, width, channels), BF16),
            pltpu.VMEM((tokens * width, channels), F32),
            pltpu.VMEM((tokens * width, channels), F32),
            pltpu.VMEM((chunks, slots, across, width, channels), BF16),
            pltpu.VMEM((chunks, G, across, stride, channels), BF16),
            dma((5,)),
            dma((5,)),
            pltpu.VMEM((HEADS * tokens, 128), F32),
            pltpu.VMEM((HEADS * tokens, 2 * tokens), F32),
            pltpu.VMEM((HEADS * tokens, channels), BF16),
            dma((chunks,)),
            dma((chunks,)),
            dma((chunks,)),
            dma((chunks,)),
            dma((4,)),
            dma((chunks,)),
        ],
        compiler_params=pltpu.CompilerParams(
            collective_id=0, has_side_effects=True, vmem_limit_bytes=58 * 1024 * 1024
        ),
    )(
        sky_map,
        expand_weight,
        expand_bias.reshape(1, wide),
        depth_weight,
        depth_bias.reshape(1, wide),
        project_weight,
        project_bias.reshape(1, channels),
        norm_gain.reshape(1, channels),
        norm_bias.reshape(1, channels),
        mixing_weight,
        position_bias,
        output_weight,
    )


def solution(mesh):
    placed = (P(("groups", "row"), "col", None),) + (P(),) * 11
    sizes = (mesh.shape["row"], mesh.shape["col"])
    return jax.shard_map(
        functools.partial(body, sizes),
        mesh=mesh,
        in_specs=placed,
        out_specs=P(("groups", "row"), "col", None),
        check_vma=False,
    )
```
